32 devices in a mesh: grp: 2 (over y), ep: 16 (over z, x, core).
Axes of the slice: x: 2, y: 2, z: 4, core: 2. Of those that a mesh axis runs over, the one named last changes fastest.
Arguments:
- resid: bfloat16 [96, 7168], P(('grp', 'ep')), parts along dimension 0, may hold values from -24 to 24
- q_latent: bfloat16 [96, 64, 512], P(('grp', 'ep')), parts along dimension 0, may hold values from -96 to 96
- q_rope: bfloat16 [96, 64, 64], P(('grp', 'ep')), parts along dimension 0, may hold values from -6 to 6
- cache_latent: bfloat16 [96, 512, 512], P(('grp', 'ep')), parts along dimension 0, may hold values from -6 to 6
- cache_rope: bfloat16 [96, 512, 64], P(('grp', 'ep')), parts along dimension 0, may hold values from -6 to 6
- lengths: int32 [96], P(('grp', 'ep')), parts along dimension 0, may hold values from 2 to 512, as said below
- proj_weight: bfloat16 [32768, 7168], P('ep'), may hold values from -0.1875 to 0.1875
- norm_gain: float32 [7168], replicated, may hold values from 0.1 to 1.9
- expert_ids: int32 [96, 2], P(('grp', 'ep')), parts along dimension 0, may hold values from 0 to 1, all different within a row; in each aligned block of 3 rows (0 to 2, 3 to 5, ...) at most 3 rows name the same one
- affinity: float32 [96, 2], P(('grp', 'ep')), parts along dimension 0, may hold values from 0.05 to 1
- w_gate: bfloat16 [16, 7168, 128], P('ep'), may hold values from -0.0625 to 0.0625
- w_up: bfloat16 [16, 7168, 128], P('ep'), may hold values from -0.0625 to 0.0625
- w_down: bfloat16 [16, 128, 7168], P('ep'), may hold values from -0.1875 to 0.1875
Outputs:
- mixed: bfloat16 [96, 7168], P(('grp', 'ep')), parts along dimension 0
The draws below stay inside these ranges and needn't reach their ends.
There are 2 independent parts, one for each index of `grp`. The reference program is written for one: setup_inputs(seed, part) draws one part's arguments, and reference() takes and returns one part's arrays. A program takes and returns all parts, laid end to end along the dimension named above; an argument that names none is the same for every part. Nothing has to cross between parts.
Inputs may be any that keep to these rules, and one draw needn't show every extreme that they name: `expert_ids`: among the 3 rows of one device (aligned blocks) no expert is named more than 3 times, a bound that some block reaches; a row names 2 different experts. `lengths`: in every draw some sequence uses all 512 positions.
All inputs are finite; a program needn't handle non-finite values.
Results may differ from the reference program's by a relative error of at most 0.0075.
Values may be sent and summed in bfloat16 or wider, within the bound.
A program may use at most 128 MiB of HBM per device.

```python
import math
import jax
import jax.numpy as jnp
import numpy as np
from jax import lax

D = 7168
HEADS = 64
LAT = 512
ROPE = 64
FF_DEV = 128
SPLIT = 8
CAP = 3
SEQ_DEV = 3
CTX = 512
FF = 1024
EXPERTS = 2
TOPK = 2
TOKENS = 48


def shared_lengths(key):
    raw_len = jax.random.randint(jax.random.fold_in(key, 501), (TOKENS,), 2, CTX + 1)
    chosen = jax.random.randint(jax.random.fold_in(key, 502), (), 0, TOKENS)
    return jnp.where(jnp.arange(TOKENS) == chosen, CTX, raw_len).astype(jnp.int32)


def shared_latent(key):
    return jnp.clip(jax.random.normal(jax.random.fold_in(key, 504), (TOKENS, CTX, LAT), jnp.float32), -6.0, 6.0)


def shared_rope(key):
    return jnp.clip(jax.random.normal(jax.random.fold_in(key, 505), (TOKENS, CTX, ROPE), jnp.float32), -6.0, 6.0)


def draw_lengths(key, part):
    base_key = key
    return shared_lengths(base_key)


def draw_cache_rope(key, part):
    base_key = key
    return shared_rope(base_key).astype(jnp.bfloat16)


def draw_cache_latent(key, part):
    base_key = key
    latent = shared_latent(base_key)
    return latent.astype(jnp.bfloat16)


def draw_q_latent(key, part):
    key = jax.random.fold_in(key, 4)
    query = jnp.clip(jax.random.normal(key, (TOKENS, HEADS, LAT), jnp.float32), -6.0, 6.0)
    return query.astype(jnp.bfloat16)


def draw_q_rope(key, part):
    key = jax.random.fold_in(key, 5)
    query = jnp.clip(jax.random.normal(key, (TOKENS, HEADS, ROPE), jnp.float32), -6.0, 6.0)
    return query.astype(jnp.bfloat16)


def draw_resid(key, part):
    key = jax.random.fold_in(key, 6)
    row_scale = jnp.exp(jax.random.uniform(jax.random.fold_in(key, 61), (TOKENS, 1), jnp.float32, math.log(0.25), math.log(2.5)))
    col_scale = jnp.exp(jax.random.uniform(jax.random.fold_in(key, 62), (1, D), jnp.float32, math.log(0.3), math.log(3.0)))
    base_val = 0.5 * jnp.clip(jax.random.normal(jax.random.fold_in(key, 64), (TOKENS, D), jnp.float32), -6.0, 6.0)
    return jnp.clip(base_val * row_scale * col_scale, -24.0, 24.0).astype(jnp.bfloat16)


def block_levels(stream_key, extent, shards, smallest, high):
    def one(position, parts):
        draws = jax.random.uniform(jax.random.fold_in(jax.random.fold_in(stream_key, 6), position), (parts,), jnp.float32, smallest / len(shards), high / len(shards))
        return jnp.repeat(jnp.exp(draws), extent[position] // parts).reshape((-1,) + (1,) * (len(extent) - position - 1))

    gain = one(*shards[0])
    for cut in shards[1:]:
        gain = gain * one(*cut)
    return gain


def routed_block(rng, own, number, rows, amount, top, limit, skew):
    ranking = jax.random.permutation(rng, amount)
    heavy_load, ordinary = shares(amount, rows * top, limit, skew, True), shares(amount, rows * top, limit, skew, False)
    places = jnp.arange(amount)

    def named(sizes, turn):
        used = int((sizes > 0).sum())
        fixed = max(1, used // 4)
        passed = fixed + (places - fixed + turn * (used - fixed)) % max(1, amount - fixed)
        return jnp.zeros((amount,), jnp.int32).at[ranking[jnp.where(places < fixed, places, passed)]].set(jnp.asarray(sizes, jnp.int32))

    sizes = jnp.where(number % 4 == 0, named(heavy_load, number // 4), named(ordinary, number - number // 4 - 1))
    mixed = jax.random.permutation(jax.random.fold_in(own, 3), amount)
    giver, sink = mixed[0:amount // 2 * 2:2], mixed[1:amount // 2 * 2:2]
    margin = jnp.minimum(sizes[giver] - 1, limit - sizes[sink]) // 2
    margin = jnp.where((giver == ranking[0]) | (sink == ranking[0]) | (sizes[sink] == 0), 0, jnp.maximum(margin, 0))
    passed = jax.random.randint(jax.random.fold_in(own, 4), (amount // 2,), 0, 1 << 20) % (margin + 1)
    sizes = sizes.at[giver].add(-passed).at[sink].add(passed)
    items = jnp.searchsorted(jnp.cumsum(sizes), jnp.arange(rows * top), side="right").astype(jnp.int32)
    grid = items.reshape(top, rows).T
    grid = grid[jax.random.permutation(jax.random.fold_in(own, 1), rows)]
    turn = jax.random.randint(jax.random.fold_in(own, 2), (rows, 1), 0, top)
    return jnp.take_along_axis(grid, (jnp.arange(top)[None, :] + turn) % top, axis=1)


def shares(count, total, limit, lean, full):
    weights = [(1 << 20) // math.isqrt(standing ** lean) + 1 for standing in range(1, count + 1)]
    largest = limit if full else min(limit, max(-(-total // count), total * weights[0] // sum(weights)))
    least = 1 if total - largest >= count - 1 else 0
    given, rest = [largest] + [least] * (count - 1), total - largest - least * (count - 1)
    while rest > 0:
        movable = [i for i in range(1, count) if given[i] < largest] or [i for i in range(1, count) if given[i] < limit]
        pool, remaining = sum([weights[i] for i in movable]), rest
        for i in movable:
            addition = min(limit - given[i], max(1, remaining * weights[i] // pool), rest)
            given[i] = given[i] + addition
            rest = rest - addition
    return np.array(given)


def scatter_about(rng, dims, width, bound, split=(), kind=jnp.bfloat16):
    level = block_levels(rng, dims, split, -0.22, 0.18) if split else 1.0
    values = jax.random.normal(rng, dims, jnp.float32) * width * level
    return jnp.minimum(jnp.maximum(values, -bound), bound).astype(kind)


def setup_inputs(seed: int = 0, part: int = 0) -> dict:
    splits = jax.random.split(jax.random.key(seed), 14)
    part_keys = jax.random.split(jax.random.fold_in(splits[13], part), 14)
    resid = draw_resid(jax.random.fold_in(jax.random.fold_in(splits[13], part), 71), part)
    q_latent = draw_q_latent(jax.random.fold_in(jax.random.fold_in(splits[13], part), 71), part)
    q_rope = draw_q_rope(jax.random.fold_in(jax.random.fold_in(splits[13], part), 71), part)
    cache_latent = draw_cache_latent(jax.random.fold_in(jax.random.fold_in(splits[13], part), 71), part)
    cache_rope = draw_cache_rope(jax.random.fold_in(jax.random.fold_in(splits[13], part), 71), part)
    lengths = draw_lengths(jax.random.fold_in(jax.random.fold_in(splits[13], part), 71), part)
    proj_weight = scatter_about(splits[6], (HEADS * LAT, D), (HEADS * LAT // 32) ** -0.5, 0.1875, ((0, 16),))
    norm_gain = jnp.clip(1.0 + 0.18 * jax.random.normal(splits[7], (D,), jnp.float32), 0.1, 1.9)
    expert_ids_keys = jax.random.split(jax.random.fold_in(part_keys[8], 1), TOKENS // SEQ_DEV)
    expert_ids_turns = jax.random.permutation(jax.random.fold_in(part_keys[8], 3), TOKENS // SEQ_DEV)
    expert_ids = jax.vmap(lambda own, number: routed_block(jax.random.fold_in(part_keys[8], 2), own, number, SEQ_DEV, EXPERTS, TOPK, CAP, 2))(expert_ids_keys, expert_ids_turns).reshape((TOKENS, TOPK))
    affinity = jnp.clip(jnp.exp(math.log(1.0) - 2.9957323 * jax.random.uniform(part_keys[9], (TOKENS, TOPK), jnp.float32) ** block_levels(part_keys[9], (TOKENS, TOPK), ((0, 16),), -0.2, 0.2)), 0.05, 1.0)
    w_gate = scatter_about(splits[10], (EXPERTS * SPLIT, D, FF_DEV), D ** -0.5, 0.0625, ((0, 16),))
    w_up = scatter_about(splits[11], (EXPERTS * SPLIT, D, FF_DEV), D ** -0.5, 0.0625, ((0, 16),))
    w_down = scatter_about(splits[12], (EXPERTS * SPLIT, FF_DEV, D), FF ** -0.5, 0.1875, ((0, 16),))
    return {"resid": resid, "q_latent": q_latent, "q_rope": q_rope, "cache_latent": cache_latent, "cache_rope": cache_rope, "lengths": lengths, "proj_weight": proj_weight, "norm_gain": norm_gain, "expert_ids": expert_ids, "affinity": affinity, "w_gate": w_gate, "w_up": w_up, "w_down": w_down}


score_scale = 0.07216878364870322
route_factor = 2.5
norm_eps = 1e-06

def reference(resid, q_latent, q_rope, cache_latent, cache_rope, lengths, proj_weight, norm_gain, expert_ids, affinity, w_gate, w_up, w_down):
    positions = jnp.arange(CTX, dtype=jnp.int32)

    def attend(packed):
        query_lat, query_rope, keys_lat, keys_rope, length = packed
        scores = jnp.einsum('hc,lc->hl', query_lat.astype(jnp.float32), keys_lat.astype(jnp.float32))
        scores = (scores + jnp.einsum('hr,lr->hl', query_rope.astype(jnp.float32), keys_rope.astype(jnp.float32))) * score_scale
        valid_mask = positions[None, :] < length
        scores = jnp.where(valid_mask, scores, -1e+30)
        peak_score = lax.optimization_barrier(jnp.max(scores, axis=1, keepdims=True))
        exponent = jnp.where(valid_mask, jnp.exp(scores - peak_score), 0.0)
        attention_weight = (exponent / lax.optimization_barrier(jnp.sum(exponent, axis=1, keepdims=True))).astype(jnp.bfloat16)
        return jnp.einsum('hl,lc->hc', attention_weight.astype(jnp.float32), keys_lat.astype(jnp.float32)).astype(jnp.bfloat16)
    heads_out = lax.map(attend, (q_latent, q_rope, cache_latent, cache_rope, lengths))
    attention = jnp.dot(heads_out.reshape(TOKENS, HEADS * LAT), proj_weight, preferred_element_type=jnp.float32)
    hidden = resid.astype(jnp.float32) + attention
    normed = (hidden * lax.rsqrt(lax.optimization_barrier(jnp.mean(hidden * hidden, axis=1, keepdims=True)) + norm_eps) * norm_gain).astype(jnp.bfloat16)
    route_weight = route_factor * affinity / lax.optimization_barrier(jnp.sum(affinity, axis=1, keepdims=True))
    gate_full = w_gate.reshape(EXPERTS, SPLIT, D, FF_DEV).transpose(0, 2, 1, 3).reshape(EXPERTS, D, FF)
    up_full = w_up.reshape(EXPERTS, SPLIT, D, FF_DEV).transpose(0, 2, 1, 3).reshape(EXPERTS, D, FF)
    down_full = w_down.reshape(EXPERTS, FF, D)

    def one_expert(carry, packed):
        expert_index, gate_mat, up_mat, down_mat = packed
        gate_val = jnp.dot(normed, gate_mat, preferred_element_type=jnp.float32)
        up_val = jnp.dot(normed, up_mat, preferred_element_type=jnp.float32)
        active = (jax.nn.silu(gate_val) * up_val).astype(jnp.bfloat16)
        result = jnp.dot(active, down_mat, preferred_element_type=jnp.float32).astype(jnp.bfloat16)
        result = lax.optimization_barrier(result).astype(jnp.float32)
        coeff = lax.optimization_barrier(jnp.sum(jnp.where(expert_ids == expert_index, route_weight, 0.0), axis=1))
        return (carry + coeff[:, None] * result, None)
    start_sum = jnp.zeros((TOKENS, D), jnp.float32)
    mixture, unused = lax.scan(one_expert, start_sum, (jnp.arange(EXPERTS, dtype=jnp.int32), gate_full, up_full, down_full))
    return (hidden + mixture).astype(jnp.bfloat16)
```

```python
import jax
import jax.numpy as jnp
from jax import lax
from jax.sharding import PartitionSpec as P

SPLIT = 8


score_scale = 0.07216878364870322
route_factor = 2.5
norm_eps = 1e-06


def scatter_sum(partial):
    devices = lax.axis_size("ep")
    blocks = partial.astype(jnp.bfloat16).reshape(devices, -1, partial.shape[1])
    arrived = lax.all_to_all(blocks, "ep", split_axis=0, concat_axis=0, tiled=True)
    return jnp.sum(arrived.astype(jnp.float32), axis=0)


def local(
    resid,
    q_latent,
    q_rope,
    cache_latent,
    cache_rope,
    lengths,
    proj_weight,
    norm_gain,
    expert_ids,
    affinity,
    w_gate,
    w_up,
    w_down,
):
    seq_count = resid.shape[0]
    ctx_len = cache_latent.shape[1]
    devices = lax.axis_size("ep")
    experts_all = devices // SPLIT
    route_weight = route_factor * affinity / jnp.sum(affinity, axis=1, keepdims=True)
    expert_cols = jnp.arange(experts_all, dtype=jnp.int32)
    named = expert_ids[:, :, None] == expert_cols
    spread = jnp.sum(jnp.where(named, route_weight[:, :, None], 0.0), axis=1)
    spread = lax.all_to_all(
        jnp.repeat(spread.T, SPLIT, axis=0), "ep", split_axis=0, concat_axis=0, tiled=True
    )
    coeff = spread.reshape(-1)
    chosen = coeff != 0.0
    scores = jnp.einsum("thc,tlc->thl", q_latent, cache_latent, preferred_element_type=jnp.float32)
    scores = (
        scores + jnp.einsum("thr,tlr->thl", q_rope, cache_rope, preferred_element_type=jnp.float32)
    ) * score_scale
    positions = jnp.arange(ctx_len, dtype=jnp.int32)
    valid_mask = positions[None, None, :] < lengths[:, None, None]
    scores = jnp.where(valid_mask, scores, -1e30)
    peak_score = jnp.max(scores, axis=2, keepdims=True)
    exponent = jnp.where(valid_mask, jnp.exp(scores - peak_score), 0.0)
    attention_weight = (exponent / jnp.sum(exponent, axis=2, keepdims=True)).astype(jnp.bfloat16)
    heads_out = jnp.einsum(
        "thl,tlc->thc", attention_weight, cache_latent, preferred_element_type=jnp.float32
    ).astype(jnp.bfloat16)
    flat_heads = heads_out.reshape(seq_count, -1)
    incoming = lax.all_to_all(flat_heads, "ep", split_axis=1, concat_axis=0, tiled=True)
    row_block = incoming
    attention = scatter_sum(jnp.dot(row_block, proj_weight, preferred_element_type=jnp.float32))
    hidden = resid.astype(jnp.float32) + attention
    normed = (
        hidden * lax.rsqrt(jnp.mean(hidden * hidden, axis=1, keepdims=True) + norm_eps) * norm_gain
    ).astype(jnp.bfloat16)
    row_block = lax.all_gather(normed, "ep", axis=0, tiled=True)
    gate_val = jnp.dot(row_block, w_gate[0], preferred_element_type=jnp.float32)
    up_val = jnp.dot(row_block, w_up[0], preferred_element_type=jnp.float32)
    active = (jax.nn.silu(gate_val) * up_val).astype(jnp.bfloat16)
    partial_value = jnp.dot(active, w_down[0], preferred_element_type=jnp.float32)
    mixture = scatter_sum(jnp.where(chosen[:, None], partial_value * coeff[:, None], 0.0))
    return (hidden + mixture).astype(jnp.bfloat16)


def solution(mesh):
    placed = (
        P(("grp", "ep"), None),
        P(("grp", "ep"), None, None),
        P(("grp", "ep"), None, None),
        P(("grp", "ep"), None, None),
        P(("grp", "ep"), None, None),
        P(("grp", "ep")),
        P("ep", None),
        P(),
        P(("grp", "ep"), None),
        P(("grp", "ep"), None),
        P("ep", None, None),
        P("ep", None, None),
        P("ep", None, None),
    )
    return jax.shard_map(
        local, mesh=mesh, in_specs=placed, out_specs=P(("grp", "ep"), None), check_vma=False
    )
```

```python
import functools

import jax
import jax.numpy as jnp
from jax import lax
from jax.experimental import pallas as pl
from jax.experimental.pallas import tpu as pltpu
from jax.sharding import PartitionSpec as P

SPLIT = 8
SLOT = 4
PARTS = 8


score_scale = 0.07216878364870322
route_factor = 2.5
norm_eps = 1e-06


def place(n):
    me = lax.axis_index("ep")
    core, side, outer = me % 2, (me // 2) % 2, me // 4
    return me, core, side, outer, core * (n // 2) + side * (n // 4) + outer


def greet(partners):
    barrier = pltpu.get_barrier_semaphore()
    for other in partners:
        pl.semaphore_signal(
            barrier, inc=1, device_id={"ep": other}, device_id_type=pl.DeviceIdType.MESH
        )
    pl.semaphore_wait(barrier, len(partners))


def send(src, dst, send_sem, recv_sem, other):
    copy = pltpu.make_async_remote_copy(
        src_ref=src,
        dst_ref=dst,
        send_sem=send_sem,
        recv_sem=recv_sem,
        device_id={"ep": other},
        device_id_type=pl.DeviceIdType.MESH,
    )
    copy.start()
    return copy


def row_picker(n, quarter):
    row = lax.broadcasted_iota(jnp.int32, (SLOT * n, 16 * n), 0)
    col = lax.broadcasted_iota(jnp.int32, (SLOT * n, 16 * n), 1)
    return (col == ((row >> 2) << 4) + (row & 3) + 4 * quarter).astype(jnp.bfloat16)


def scatter_sum(n, product, out_ref, own, leave, first, leave2, second, block, third, sems):
    me, core, side, outer, slot = place(n)
    rows = SLOT * n
    outers = n // 4
    send1, recv1, send2, recv2, send3, recv3 = sems
    copies1, copies2, copies3 = {}, {}, []
    width = out_ref.shape[2]
    sums = {}

    def half(value):
        return pl.ds(pl.multiple_of(value * (rows // 2), 16), rows // 2)

    def quarter(value):
        return pl.ds(pl.multiple_of(value * (rows // 4), 16), rows // 4)

    def begin(part):
        value = product(part)
        own[part] = value
        leave[part] = value.astype(jnp.bfloat16)
        copies1[part] = send(
            leave.at[part, half(1 - core)],
            first.at[part],
            send1.at[part],
            recv1.at[part],
            me + 1 - 2 * core,
        )

    def over_x(part):
        copies1[part].wait_recv()
        value = own[part, half(core)] + first[part].astype(jnp.float32)
        own[part, half(core)] = value
        leave2[part] = value.astype(jnp.bfloat16)
        copies2[part] = send(
            leave2.at[part, quarter(1 - side)],
            second.at[part],
            send2.at[part],
            recv2.at[part],
            me + 2 - 4 * side,
        )

    def over_rest(part):
        copies2[part].wait_recv()
        value = own[part, quarter(2 * core + side)] + second[part].astype(jnp.float32)
        sums[part] = value.astype(jnp.bfloat16)
        if part % 4 < 3:
            return
        group = part // 4
        row = lax.broadcasted_iota(jnp.int32, (16 * outers, rows // 4), 0)
        col = lax.broadcasted_iota(jnp.int32, (16 * outers, rows // 4), 1)
        total = jnp.zeros((16 * outers, width), jnp.float32)
        for j in range(4):
            pick = (((row >> 2) & 3) == j) & (col == ((row >> 4) << 2) + (row & 3))
            total = total + jnp.dot(
                pick.astype(jnp.bfloat16), sums[group * 4 + j], preferred_element_type=jnp.float32
            )
        block[group] = total.astype(jnp.bfloat16).reshape(outers, 16, width)
        for d in range(1, outers):
            there = lax.rem(outer + d, outers)
            copies3.append(
                send(
                    block.at[group, there],
                    third.at[group, d - 1],
                    send3.at[group, d - 1],
                    recv3.at[group, d - 1],
                    there * 4 + side * 2 + core,
                )
            )

    for step in range(PARTS + 2):
        if step < PARTS:
            begin(step)
        if 1 <= step <= PARTS:
            over_x(step - 1)
        if step >= 2:
            over_rest(step - 2)
    for group in range(2):
        value = block[group, outer].astype(jnp.float32)
        for d in range(1, outers):
            copies3[group * (outers - 1) + d - 1].wait_recv()
            value = value + third[group, d - 1].astype(jnp.float32)
        out_ref[group] = value
    for copy in [*copies1.values(), *copies2.values(), *copies3]:
        copy.wait_send()


def sum_scratch(n, width):
    rows, outers = SLOT * n, n // 4
    dma = pltpu.SemaphoreType.DMA
    return [
        pltpu.VMEM((PARTS, rows, width), jnp.float32),
        pltpu.VMEM((PARTS, rows, width), jnp.bfloat16),
        pltpu.VMEM((PARTS, rows // 2, width), jnp.bfloat16),
        pltpu.VMEM((PARTS, rows // 2, width), jnp.bfloat16),
        pltpu.VMEM((PARTS, rows // 4, width), jnp.bfloat16),
        pltpu.VMEM((2, outers, 16, width), jnp.bfloat16),
        pltpu.VMEM((2, outers - 1, 16, width), jnp.bfloat16),
        dma((PARTS,)),
        dma((PARTS,)),
        dma((PARTS,)),
        dma((PARTS,)),
        dma((2, outers - 1)),
        dma((2, outers - 1)),
    ]


def project_kernel(
    n, heads_ref, weight_ref, out_ref, arrived, lhs, weight, send_sem, recv_sem, load_sem, *rest
):
    me, core, side, outer, slot = place(n)
    width = out_ref.shape[2]
    quarter = heads_ref.shape[2]
    loads = []
    for part in range(PARTS):
        load = pltpu.make_async_copy(
            weight_ref.at[:, pl.ds(part * width, width)], weight.at[part], load_sem.at[part]
        )
        load.start()
        loads.append(load)
    greet([lax.rem(me + d, n) for d in range(1, n)])
    copies = []
    for d in range(1, n):
        other = lax.rem(me + d, n)
        copies.append(
            send(
                heads_ref.at[other],
                arrived.at[slot],
                send_sem.at[d - 1],
                recv_sem.at[d - 1],
                other,
            )
        )
    arrived[slot] = heads_ref[me]
    for copy in copies:
        copy.wait_recv()
    rows = arrived[...].reshape(16 * n, quarter)
    for q in range(4):
        lhs[q] = jnp.dot(row_picker(n, q), rows, preferred_element_type=jnp.float32).astype(
            jnp.bfloat16
        )

    def product(part):
        loads[part].wait()
        total = jnp.zeros((SLOT * n, width), jnp.float32)
        for q in range(4):
            total = total + jnp.dot(
                lhs[q],
                weight[part, pl.ds(q * quarter, quarter)],
                preferred_element_type=jnp.float32,
            )
        return total

    scatter_sum(n, product, out_ref, *rest[:7], rest[7:])
    for copy in copies:
        copy.wait_send()


def expert_kernel(
    n, normed_ref, coeff_ref, gate_ref, up_ref, down_ref, out_ref,
    gathered, gate, up, down, load_sem, send_a, recv_a, send_b, recv_b, send_c, recv_c, *rest
):
    me, core, side, outer, slot = place(n)
    width = out_ref.shape[2]
    outers = n // 4
    quarter = normed_ref.shape[1]
    loads = []
    for i, (src, dst) in enumerate(((gate_ref, gate), (up_ref, up), (down_ref, down))):
        load = pltpu.make_async_copy(src, dst, load_sem.at[i])
        load.start()
        loads.append(load)
    across, sibling = me + 2 - 4 * side, me + 1 - 2 * core
    peers = [lax.rem(outer + d, outers) * 4 + side * 2 + core for d in range(1, outers)]
    greet([*peers, across, sibling])
    gathered[slot] = normed_ref[...]
    along = []
    for d in range(1, outers):
        along.append(
            send(normed_ref, gathered.at[slot], send_a.at[d - 1], recv_a.at[d - 1], peers[d - 1])
        )
    over, core_copies = [], []
    for d in range(outers):
        if d:
            along[d - 1].wait_recv()
        index = core * (n // 2) + side * (n // 4) + lax.rem(outer - d + outers, outers)
        held = gathered.at[index]
        over.append(send(held, held, send_b.at[d], recv_b.at[d], across))
        core_copies.append(send(held, held, send_c.at[d], recv_c.at[d], sibling))
    for d in range(outers):
        over[d].wait_recv()
        index = core * (n // 2) + (1 - side) * (n // 4) + lax.rem(outer - d + outers, outers)
        held = gathered.at[index]
        core_copies.append(
            send(held, held, send_c.at[outers + d], recv_c.at[outers + d], sibling)
        )
    for copy in core_copies:
        copy.wait_recv()
    loads[0].wait()
    loads[1].wait()
    rows = gathered[...].reshape(16 * n, quarter)
    gate_val = jnp.zeros((SLOT * n, gate.shape[1]), jnp.float32)
    up_val = jnp.zeros((SLOT * n, gate.shape[1]), jnp.float32)
    for q in range(4):
        lhs = jnp.dot(row_picker(n, q), rows, preferred_element_type=jnp.float32).astype(
            jnp.bfloat16
        )
        span = pl.ds(q * quarter, quarter)
        gate_val = gate_val + jnp.dot(lhs, gate[span], preferred_element_type=jnp.float32)
        up_val = up_val + jnp.dot(lhs, up[span], preferred_element_type=jnp.float32)
    active = (gate_val / (1.0 + jnp.exp(-gate_val)) * up_val).astype(jnp.bfloat16)
    coeff = coeff_ref[...]
    loads[2].wait()

    def product(part):
        value = jnp.dot(
            active, down[:, pl.ds(part * width, width)], preferred_element_type=jnp.float32
        )
        return jnp.where(coeff != 0.0, value * coeff, 0.0)

    scatter_sum(n, product, out_ref, *rest[:7], rest[7:])
    for copy in [*along, *over, *core_copies]:
        copy.wait_send()


def slot_order(value, n):
    rest = value.shape[1:]
    return value.reshape(n // 4, 2, 2, *rest).swapaxes(0, 2).reshape(n, *rest)


def unfold(summed, seq_count):
    width = summed.shape[2]
    split = summed.reshape(2, 4, SLOT, width).transpose(2, 0, 1, 3)
    return split.reshape(SLOT, PARTS * width)[:seq_count]


def project(flat_heads, weight):
    n = lax.axis_size("ep")
    depth, model_width = weight.shape
    seq_count = flat_heads.shape[0]
    quarter, width = depth // 4, model_width // PARTS
    padded = jnp.pad(flat_heads, ((0, SLOT - seq_count), (0, 0)))
    blocks = padded.reshape(SLOT, n, 4, quarter).transpose(1, 2, 0, 3).reshape(n, 16, quarter)
    vmem = pl.BlockSpec(memory_space=pltpu.VMEM)
    dma = pltpu.SemaphoreType.DMA
    summed = pl.pallas_call(
        functools.partial(project_kernel, n),
        out_shape=jax.ShapeDtypeStruct((2, 16, width), jnp.float32),
        in_specs=[vmem, pl.BlockSpec(memory_space=pl.ANY)],
        out_specs=vmem,
        scratch_shapes=[
            pltpu.VMEM((n, 16, quarter), jnp.bfloat16),
            pltpu.VMEM((4, SLOT * n, quarter), jnp.bfloat16),
            pltpu.VMEM((PARTS, depth, width), jnp.bfloat16),
            dma((n - 1,)),
            dma((n - 1,)),
            dma((PARTS,)),
            *sum_scratch(n, width),
        ],
        compiler_params=pltpu.CompilerParams(
            collective_id=0, has_side_effects=True, vmem_limit_bytes=56 * 2**20
        ),
    )(blocks, weight)
    return unfold(summed, seq_count)


def experts(normed, coeff, w_gate, w_up, w_down):
    n = lax.axis_size("ep")
    seq_count, model_width = normed.shape
    hidden_width = w_gate.shape[1]
    quarter, width = model_width // 4, model_width // PARTS
    outers = n // 4
    padded = jnp.pad(normed, ((0, SLOT - seq_count), (0, 0)))
    block = padded.reshape(SLOT, 4, quarter).transpose(1, 0, 2).reshape(16, quarter)
    weights = jnp.pad(slot_order(coeff, n), ((0, 0), (0, SLOT - seq_count)))
    vmem = pl.BlockSpec(memory_space=pltpu.VMEM)
    hbm = pl.BlockSpec(memory_space=pl.ANY)
    dma = pltpu.SemaphoreType.DMA
    summed = pl.pallas_call(
        functools.partial(expert_kernel, n),
        out_shape=jax.ShapeDtypeStruct((2, 16, width), jnp.float32),
        in_specs=[vmem, vmem, hbm, hbm, hbm],
        out_specs=vmem,
        scratch_shapes=[
            pltpu.VMEM((n, 16, quarter), jnp.bfloat16),
            pltpu.VMEM((model_width, hidden_width), jnp.bfloat16),
            pltpu.VMEM((model_width, hidden_width), jnp.bfloat16),
            pltpu.VMEM((hidden_width, model_width), jnp.bfloat16),
            dma((3,)),
            dma((outers - 1,)),
            dma((outers - 1,)),
            dma((outers,)),
            dma((outers,)),
            dma((2 * outers,)),
            dma((2 * outers,)),
            *sum_scratch(n, width),
        ],
        compiler_params=pltpu.CompilerParams(
            collective_id=1, has_side_effects=True, vmem_limit_bytes=56 * 2**20
        ),
    )(block, weights.reshape(SLOT * n, 1), w_gate, w_up, w_down)
    return unfold(summed, seq_count)


def local(
    resid,
    q_latent,
    q_rope,
    cache_latent,
    cache_rope,
    lengths,
    proj_weight,
    norm_gain,
    expert_ids,
    affinity,
    w_gate,
    w_up,
    w_down,
):
    seq_count = resid.shape[0]
    ctx_len = cache_latent.shape[1]
    devices = lax.axis_size("ep")
    experts_all = devices // SPLIT
    route_weight = route_factor * affinity / jnp.sum(affinity, axis=1, keepdims=True)
    expert_cols = jnp.arange(experts_all, dtype=jnp.int32)
    named = expert_ids[:, :, None] == expert_cols
    spread = jnp.sum(jnp.where(named, route_weight[:, :, None], 0.0), axis=1)
    spread = lax.all_to_all(
        jnp.repeat(spread.T, SPLIT, axis=0), "ep", split_axis=0, concat_axis=0, tiled=True
    )
    coeff = spread.reshape(devices, seq_count)
    scores = jnp.einsum("thc,tlc->thl", q_latent, cache_latent, preferred_element_type=jnp.float32)
    scores = (
        scores + jnp.einsum("thr,tlr->thl", q_rope, cache_rope, preferred_element_type=jnp.float32)
    ) * score_scale
    positions = jnp.arange(ctx_len, dtype=jnp.int32)
    valid_mask = positions[None, None, :] < lengths[:, None, None]
    scores = jnp.where(valid_mask, scores, -1e30)
    peak_score = jnp.max(scores, axis=2, keepdims=True)
    exponent = jnp.where(valid_mask, jnp.exp(scores - peak_score), 0.0)
    attention_weight = (exponent / jnp.sum(exponent, axis=2, keepdims=True)).astype(jnp.bfloat16)
    heads_out = jnp.einsum(
        "thl,tlc->thc", attention_weight, cache_latent, preferred_element_type=jnp.float32
    ).astype(jnp.bfloat16)
    flat_heads = heads_out.reshape(seq_count, -1)
    attention = project(flat_heads, proj_weight)
    hidden = resid.astype(jnp.float32) + attention
    normed = (
        hidden * lax.rsqrt(jnp.mean(hidden * hidden, axis=1, keepdims=True) + norm_eps) * norm_gain
    ).astype(jnp.bfloat16)
    mixture = experts(normed, coeff, w_gate[0], w_up[0], w_down[0])
    return (hidden + mixture).astype(jnp.bfloat16)


def solution(mesh):
    placed = (
        P(("grp", "ep"), None),
        P(("grp", "ep"), None, None),
        P(("grp", "ep"), None, None),
        P(("grp", "ep"), None, None),
        P(("grp", "ep"), None, None),
        P(("grp", "ep")),
        P("ep", None),
        P(),
        P(("grp", "ep"), None),
        P(("grp", "ep"), None),
        P("ep", None, None),
        P("ep", None, None),
        P("ep", None, None),
    )
    return jax.shard_map(
        local, mesh=mesh, in_specs=placed, out_specs=P(("grp", "ep"), None), check_vma=False
    )
```

```python
import functools

import jax
import jax.numpy as jnp
from jax import lax
from jax.experimental import pallas as pl
from jax.experimental.pallas import tpu as pltpu
from jax.sharding import PartitionSpec as P

SPLIT = 8
SLOT = 4
LANES = 128
PARTS = 8


score_scale = 0.07216878364870322
route_factor = 2.5
norm_eps = 1e-06


def place(n):
    me = lax.axis_index("ep")
    core, side, outer = me % 2, (me // 2) % 2, me // 4
    return me, core, side, outer, core * (n // 2) + side * (n // 4) + outer


def greet(partners):
    barrier = pltpu.get_barrier_semaphore()
    for other in partners:
        pl.semaphore_signal(
            barrier, inc=1, device_id={"ep": other}, device_id_type=pl.DeviceIdType.MESH
        )
    pl.semaphore_wait(barrier, len(partners))


def send(src, dst, send_sem, recv_sem, other):
    copy = pltpu.make_async_remote_copy(
        src_ref=src,
        dst_ref=dst,
        send_sem=send_sem,
        recv_sem=recv_sem,
        device_id={"ep": other},
        device_id_type=pl.DeviceIdType.MESH,
    )
    copy.start()
    return copy


def row_picker(n, quarter):
    row = lax.broadcasted_iota(jnp.int32, (SLOT * n, 16 * n), 0)
    col = lax.broadcasted_iota(jnp.int32, (SLOT * n, 16 * n), 1)
    return (col == ((row >> 2) << 4) + (row & 3) + 4 * quarter).astype(jnp.bfloat16)


def scatter_sum(n, product, finish, lags, own, leave, first, leave2, second, block, third, sems):
    me, core, side, outer, slot = place(n)
    rows = SLOT * n
    outers = n // 4
    send1, recv1, send2, recv2, send3, recv3 = sems
    copies1, copies2, copies3 = {}, {}, []
    width = own.shape[2]
    sums = {}

    def half(value):
        return pl.ds(pl.multiple_of(value * (rows // 2), 16), rows // 2)

    def quarter(value):
        return pl.ds(pl.multiple_of(value * (rows // 4), 16), rows // 4)

    def begin(part):
        value = product(part)
        own[part] = value
        leave[part] = value.astype(jnp.bfloat16)
        copies1[part] = send(
            leave.at[part, half(1 - core)],
            first.at[part],
            send1.at[part],
            recv1.at[part],
            me + 1 - 2 * core,
        )

    def over_x(part):
        copies1[part].wait_recv()
        value = own[part, half(core)] + first[part].astype(jnp.float32)
        own[part, half(core)] = value
        leave2[part] = value.astype(jnp.bfloat16)
        copies2[part] = send(
            leave2.at[part, quarter(1 - side)],
            second.at[part],
            send2.at[part],
            recv2.at[part],
            me + 2 - 4 * side,
        )

    def over_rest(part):
        copies2[part].wait_recv()
        value = own[part, quarter(2 * core + side)] + second[part].astype(jnp.float32)
        sums[part] = value.astype(jnp.bfloat16)
        if part % 4 < 3:
            return
        group = part // 4
        row = lax.broadcasted_iota(jnp.int32, (16 * outers, rows // 4), 0)
        col = lax.broadcasted_iota(jnp.int32, (16 * outers, rows // 4), 1)
        total = jnp.zeros((16 * outers, width), jnp.float32)
        for j in range(4):
            pick = (((row >> 2) & 3) == j) & (col == ((row >> 4) << 2) + (row & 3))
            total = total + jnp.dot(
                pick.astype(jnp.bfloat16), sums[group * 4 + j], preferred_element_type=jnp.float32
            )
        block[group] = total.astype(jnp.bfloat16).reshape(outers, 16, width)
        for d in range(1, outers):
            there = lax.rem(outer + d, outers)
            copies3.append(
                send(
                    block.at[group, there],
                    third.at[group, d - 1],
                    send3.at[group, d - 1],
                    recv3.at[group, d - 1],
                    there * 4 + side * 2 + core,
                )
            )

    for step in range(PARTS + lags[1]):
        if step < PARTS:
            begin(step)
        if 0 <= step - lags[0] < PARTS:
            over_x(step - lags[0])
        if step >= lags[1]:
            over_rest(step - lags[1])
    for group in range(2):
        value = block[group, outer].astype(jnp.float32)
        for d in range(1, outers):
            copies3[group * (outers - 1) + d - 1].wait_recv()
            value = value + third[group, d - 1].astype(jnp.float32)
        finish(group, value)
    for copy in [*copies1.values(), *copies2.values(), *copies3]:
        copy.wait_send()


def sum_scratch(n, width):
    rows, outers = SLOT * n, n // 4
    dma = pltpu.SemaphoreType.DMA
    return [
        pltpu.VMEM((PARTS, rows, width), jnp.float32),
        pltpu.VMEM((PARTS, rows, width), jnp.bfloat16),
        pltpu.VMEM((PARTS, rows // 2, width), jnp.bfloat16),
        pltpu.VMEM((PARTS, rows // 2, width), jnp.bfloat16),
        pltpu.VMEM((PARTS, rows // 4, width), jnp.bfloat16),
        pltpu.VMEM((2, outers, 16, width), jnp.bfloat16),
        pltpu.VMEM((2, outers - 1, 16, width), jnp.bfloat16),
        dma((PARTS,)),
        dma((PARTS,)),
        dma((PARTS,)),
        dma((PARTS,)),
        dma((2, outers - 1)),
        dma((2, outers - 1)),
    ]


def project_kernel(
    n, heads_ref, weight_ref, out_ref, arrived, lhs, weight, send_sem, recv_sem, load_sem, *rest
):
    me, core, side, outer, slot = place(n)
    width = out_ref.shape[2]
    quarter = heads_ref.shape[2]
    loads = []
    for part in range(PARTS):
        load = pltpu.make_async_copy(
            weight_ref.at[:, pl.ds(part * width, width)], weight.at[part], load_sem.at[part]
        )
        load.start()
        loads.append(load)
    greet([lax.rem(me + d, n) for d in range(1, n)])
    copies = []
    for d in range(1, n):
        other = lax.rem(me + d, n)
        copies.append(
            send(
                heads_ref.at[other],
                arrived.at[slot],
                send_sem.at[d - 1],
                recv_sem.at[d - 1],
                other,
            )
        )
    arrived[slot] = heads_ref[me]
    for copy in copies:
        copy.wait_recv()
    rows = arrived[...].reshape(16 * n, quarter)
    for q in range(4):
        lhs[q] = jnp.dot(row_picker(n, q), rows, preferred_element_type=jnp.float32).astype(
            jnp.bfloat16
        )

    def product(part):
        loads[part].wait()
        total = jnp.zeros((SLOT * n, width), jnp.float32)
        for q in range(4):
            total = total + jnp.dot(
                lhs[q],
                weight[part, pl.ds(q * quarter, quarter)],
                preferred_element_type=jnp.float32,
            )
        return total

    def finish(group, value):
        out_ref[group] = value

    scatter_sum(n, product, finish, (2, 4), *rest[:7], rest[7:])
    for copy in copies:
        copy.wait_send()


def expert_kernel(
    n, summed_ref, resid_ref, gain_ref, tag_ref, gate_ref, up_ref, down_ref, out_ref,
    hidden, gathered, gate, up, down, load_sem, send_a, recv_a, send_b, recv_b, send_c, recv_c, *rest
):
    me, core, side, outer, slot = place(n)
    width = out_ref.shape[2]
    outers = n // 4
    loads = []
    for i, (src, dst) in enumerate(((gate_ref, gate), (up_ref, up), (down_ref, down))):
        load = pltpu.make_async_copy(src, dst, load_sem.at[i])
        load.start()
        loads.append(load)
    across, sibling = me + 2 - 4 * side, me + 1 - 2 * core
    peers = [lax.rem(outer + d, outers) * 4 + side * 2 + core for d in range(1, outers)]
    greet([*peers, across, sibling])
    squares = jnp.zeros((16, 1), jnp.float32)
    for group in range(2):
        value = summed_ref[group] + resid_ref[group]
        hidden[group] = value
        squares = squares + jnp.sum(value * value, axis=1, keepdims=True)
    total = squares[0:4] + squares[4:8] + squares[8:12] + squares[12:16]
    scale = lax.rsqrt(total / (PARTS * width) + norm_eps)
    scale = jnp.concatenate([scale] * 4, axis=0)
    for group in range(2):
        normed = (hidden[group] * scale * gain_ref[group]).astype(jnp.bfloat16)
        gathered[slot, group] = normed + tag_ref[group]
    mine = gathered.at[slot]
    along = []
    for d in range(1, outers):
        along.append(
            send(mine, mine, send_a.at[d - 1], recv_a.at[d - 1], peers[d - 1])
        )
    over, core_copies = [], []
    for d in range(outers):
        if d:
            along[d - 1].wait_recv()
        index = core * (n // 2) + side * (n // 4) + lax.rem(outer - d + outers, outers)
        held = gathered.at[index]
        over.append(send(held, held, send_b.at[d], recv_b.at[d], across))
        core_copies.append(send(held, held, send_c.at[d], recv_c.at[d], sibling))
    for d in range(outers):
        over[d].wait_recv()
        index = core * (n // 2) + (1 - side) * (n // 4) + lax.rem(outer - d + outers, outers)
        held = gathered.at[index]
        core_copies.append(
            send(held, held, send_c.at[outers + d], recv_c.at[outers + d], sibling)
        )
    for copy in core_copies:
        copy.wait_recv()
    loads[0].wait()
    loads[1].wait()
    gate_val = jnp.zeros((SLOT * n, gate.shape[1]), jnp.float32)
    up_val = jnp.zeros((SLOT * n, gate.shape[1]), jnp.float32)
    for part in range(PARTS):
        rows = gathered[:, part // 4].reshape(16 * n, width)
        lhs = jnp.dot(
            row_picker(n, part % 4), rows, preferred_element_type=jnp.float32
        ).astype(jnp.bfloat16)
        span = pl.ds(part * width, width)
        gate_val = gate_val + jnp.dot(lhs, gate[span], preferred_element_type=jnp.float32)
        up_val = up_val + jnp.dot(lhs, up[span], preferred_element_type=jnp.float32)
    row = lax.broadcasted_iota(jnp.int32, (SLOT * n, 16 * n), 0)
    col = lax.broadcasted_iota(jnp.int32, (SLOT * n, 16 * n), 1)
    tags = jnp.dot(
        (col == ((row >> 2) << 4) + 3).astype(jnp.bfloat16),
        gathered[:, 0].reshape(16 * n, width)[:, : 2 * LANES],
        preferred_element_type=jnp.float32,
    )
    row = lax.broadcasted_iota(jnp.int32, (SLOT * n, 2 * LANES), 0)
    col = lax.broadcasted_iota(jnp.int32, (SLOT * n, 2 * LANES), 1)
    wanted = (col & (LANES - 1)) == (me // SPLIT) * SLOT + (row & 3)
    coeff = jnp.sum(jnp.where(wanted, tags, 0.0), axis=1, keepdims=True)
    active = (gate_val / (1.0 + jnp.exp(-gate_val)) * up_val).astype(jnp.bfloat16)
    loads[2].wait()

    def product(part):
        value = jnp.dot(
            active, down[:, pl.ds(part * width, width)], preferred_element_type=jnp.float32
        )
        return jnp.where(coeff != 0.0, value * coeff, 0.0)

    def finish(group, value):
        out_ref[group] = (hidden[group] + value).astype(jnp.bfloat16)

    scatter_sum(n, product, finish, (PARTS, 2 * PARTS), *rest[:7], rest[7:])
    for copy in [*along, *over, *core_copies]:
        copy.wait_send()


def fold(value):
    seq_count, model_width = value.shape
    width = model_width // PARTS
    padded = jnp.pad(value, ((0, SLOT - seq_count), (0, 0)))
    return padded.reshape(SLOT, 2, 4, width).transpose(1, 2, 0, 3).reshape(2, 16, width)


def unfold(summed, seq_count):
    width = summed.shape[2]
    split = summed.reshape(2, 4, SLOT, width).transpose(2, 0, 1, 3)
    return split.reshape(SLOT, PARTS * width)[:seq_count]


def project(flat_heads, weight):
    n = lax.axis_size("ep")
    depth, model_width = weight.shape
    seq_count = flat_heads.shape[0]
    quarter, width = depth // 4, model_width // PARTS
    padded = jnp.pad(flat_heads, ((0, SLOT - seq_count), (0, 0)))
    blocks = padded.reshape(SLOT, n, 4, quarter).transpose(1, 2, 0, 3).reshape(n, 16, quarter)
    vmem = pl.BlockSpec(memory_space=pltpu.VMEM)
    dma = pltpu.SemaphoreType.DMA
    summed = pl.pallas_call(
        functools.partial(project_kernel, n),
        out_shape=jax.ShapeDtypeStruct((2, 16, width), jnp.float32),
        in_specs=[vmem, pl.BlockSpec(memory_space=pl.ANY)],
        out_specs=vmem,
        scratch_shapes=[
            pltpu.VMEM((n, 16, quarter), jnp.bfloat16),
            pltpu.VMEM((4, SLOT * n, quarter), jnp.bfloat16),
            pltpu.VMEM((PARTS, depth, width), jnp.bfloat16),
            dma((n - 1,)),
            dma((n - 1,)),
            dma((PARTS,)),
            *sum_scratch(n, width),
        ],
        compiler_params=pltpu.CompilerParams(
            collective_id=0, has_side_effects=True, vmem_limit_bytes=56 * 2**20
        ),
    )(blocks, weight)
    return summed


def experts(summed, resid, norm_gain, spread, w_gate, w_up, w_down):
    n = lax.axis_size("ep")
    seq_count, model_width = resid.shape
    hidden_width = w_gate.shape[1]
    width = model_width // PARTS
    outers = n // 4
    gain = jnp.repeat(norm_gain.reshape(2, 4, width), SLOT, axis=1)
    weights = jnp.pad(spread.T, ((0, 0), (0, SLOT - seq_count))).reshape(-1)
    weights = jnp.pad(weights, (0, LANES - weights.shape[0]))
    high = lax.reduce_precision(weights, 8, 7)
    tag_row = jnp.concatenate([high, weights - high]).astype(jnp.bfloat16)
    tags = jnp.pad(tag_row[None, None, :], ((0, 1), (3, 12), (0, width - 2 * LANES)))
    vmem = pl.BlockSpec(memory_space=pltpu.VMEM)
    hbm = pl.BlockSpec(memory_space=pl.ANY)
    dma = pltpu.SemaphoreType.DMA
    mixed = pl.pallas_call(
        functools.partial(expert_kernel, n),
        out_shape=jax.ShapeDtypeStruct((2, 16, width), jnp.bfloat16),
        in_specs=[vmem, vmem, vmem, vmem, hbm, hbm, hbm],
        out_specs=vmem,
        scratch_shapes=[
            pltpu.VMEM((2, 16, width), jnp.float32),
            pltpu.VMEM((n, 2, 16, width), jnp.bfloat16),
            pltpu.VMEM((model_width, hidden_width), jnp.bfloat16),
            pltpu.VMEM((model_width, hidden_width), jnp.bfloat16),
            pltpu.VMEM((hidden_width, model_width), jnp.bfloat16),
            dma((3,)),
            dma((outers - 1,)),
            dma((outers - 1,)),
            dma((outers,)),
            dma((outers,)),
            dma((2 * outers,)),
            dma((2 * outers,)),
            *sum_scratch(n, width),
        ],
        compiler_params=pltpu.CompilerParams(
            collective_id=1, has_side_effects=True, vmem_limit_bytes=56 * 2**20
        ),
    )(summed, fold(resid.astype(jnp.float32)), gain, tags, w_gate, w_up, w_down)
    return unfold(mixed, seq_count)


def local(
    resid,
    q_latent,
    q_rope,
    cache_latent,
    cache_rope,
    lengths,
    proj_weight,
    norm_gain,
    expert_ids,
    affinity,
    w_gate,
    w_up,
    w_down,
):
    seq_count = resid.shape[0]
    ctx_len = cache_latent.shape[1]
    devices = lax.axis_size("ep")
    experts_all = devices // SPLIT
    route_weight = route_factor * affinity / jnp.sum(affinity, axis=1, keepdims=True)
    expert_cols = jnp.arange(experts_all, dtype=jnp.int32)
    named = expert_ids[:, :, None] == expert_cols
    spread = jnp.sum(jnp.where(named, route_weight[:, :, None], 0.0), axis=1)
    scores = jnp.einsum("thc,tlc->thl", q_latent, cache_latent, preferred_element_type=jnp.float32)
    scores = (
        scores + jnp.einsum("thr,tlr->thl", q_rope, cache_rope, preferred_element_type=jnp.float32)
    ) * score_scale
    positions = jnp.arange(ctx_len, dtype=jnp.int32)
    valid_mask = positions[None, None, :] < lengths[:, None, None]
    scores = jnp.where(valid_mask, scores, -1e30)
    peak_score = jnp.max(scores, axis=2, keepdims=True)
    exponent = jnp.where(valid_mask, jnp.exp(scores - peak_score), 0.0)
    attention_weight = (exponent / jnp.sum(exponent, axis=2, keepdims=True)).astype(jnp.bfloat16)
    heads_out = jnp.einsum(
        "thl,tlc->thc", attention_weight, cache_latent, preferred_element_type=jnp.float32
    ).astype(jnp.bfloat16)
    flat_heads = heads_out.reshape(seq_count, -1)
    summed = project(flat_heads, proj_weight)
    return experts(summed, resid, norm_gain, spread, w_gate[0], w_up[0], w_down[0])


def solution(mesh):
    placed = (
        P(("grp", "ep"), None),
        P(("grp", "ep"), None, None),
        P(("grp", "ep"), None, None),
        P(("grp", "ep"), None, None),
        P(("grp", "ep"), None, None),
        P(("grp", "ep")),
        P("ep", None),
        P(),
        P(("grp", "ep"), None),
        P(("grp", "ep"), None),
        P("ep", None, None),
        P("ep", None, None),
        P("ep", None, None),
    )
    return jax.shard_map(
        local, mesh=mesh, in_specs=placed, out_specs=P(("grp", "ep"), None), check_vma=False
    )
```

```python
import functools

import jax
import jax.numpy as jnp
from jax import lax
from jax.experimental import pallas as pl
from jax.experimental.pallas import tpu as pltpu
from jax.sharding import PartitionSpec as P

SPLIT = 8
SLOT = 4
LANES = 128
PARTS = 8


score_scale = 0.07216878364870322
route_factor = 2.5
norm_eps = 1e-06


def place(n):
    me = lax.axis_index("ep")
    core, side, outer = me % 2, (me // 2) % 2, me // 4
    return me, core, side, outer, core * (n // 2) + side * (n // 4) + outer


def greet(partners):
    barrier = pltpu.get_barrier_semaphore()
    for other in partners:
        pl.semaphore_signal(
            barrier, inc=1, device_id={"ep": other}, device_id_type=pl.DeviceIdType.MESH
        )
    pl.semaphore_wait(barrier, len(partners))


def send(src, dst, send_sem, recv_sem, other):
    copy = pltpu.make_async_remote_copy(
        src_ref=src,
        dst_ref=dst,
        send_sem=send_sem,
        recv_sem=recv_sem,
        device_id={"ep": other},
        device_id_type=pl.DeviceIdType.MESH,
    )
    copy.start()
    return copy


def row_picker(n, quarter):
    row = lax.broadcasted_iota(jnp.int32, (SLOT * n, 16 * n), 0)
    col = lax.broadcasted_iota(jnp.int32, (SLOT * n, 16 * n), 1)
    return (col == ((row >> 2) << 4) + (row & 3) + 4 * quarter).astype(jnp.bfloat16)


def scatter_sum(n, product, finish, lags, own, leave, first, leave2, second, block, third, sems):
    me, core, side, outer, slot = place(n)
    rows = SLOT * n
    outers = n // 4
    send1, recv1, send2, recv2, send3, recv3 = sems
    copies1, copies2, copies3 = {}, {}, []
    width = own.shape[2]
    sums = {}

    def half(value):
        return pl.ds(pl.multiple_of(value * (rows // 2), 16), rows // 2)

    def quarter(value):
        return pl.ds(pl.multiple_of(value * (rows // 4), 16), rows // 4)

    def begin(part):
        value = product(part)
        own[part] = value
        leave[part] = value.astype(jnp.bfloat16)
        copies1[part] = send(
            leave.at[part, half(1 - core)],
            first.at[part],
            send1.at[part],
            recv1.at[part],
            me + 1 - 2 * core,
        )

    def over_x(part):
        copies1[part].wait_recv()
        value = own[part, half(core)] + first[part].astype(jnp.float32)
        own[part, half(core)] = value
        leave2[part] = value.astype(jnp.bfloat16)
        copies2[part] = send(
            leave2.at[part, quarter(1 - side)],
            second.at[part],
            send2.at[part],
            recv2.at[part],
            me + 2 - 4 * side,
        )

    def over_rest(part):
        copies2[part].wait_recv()
        value = own[part, quarter(2 * core + side)] + second[part].astype(jnp.float32)
        sums[part] = value.astype(jnp.bfloat16)
        if part % 4 < 3:
            return
        group = part // 4
        row = lax.broadcasted_iota(jnp.int32, (16 * outers, rows // 4), 0)
        col = lax.broadcasted_iota(jnp.int32, (16 * outers, rows // 4), 1)
        total = jnp.zeros((16 * outers, width), jnp.float32)
        for j in range(4):
            pick = (((row >> 2) & 3) == j) & (col == ((row >> 4) << 2) + (row & 3))
            total = total + jnp.dot(
                pick.astype(jnp.bfloat16), sums[group * 4 + j], preferred_element_type=jnp.float32
            )
        block[group] = total.astype(jnp.bfloat16).reshape(outers, 16, width)
        for d in range(1, outers):
            there = lax.rem(outer + d, outers)
            copies3.append(
                send(
                    block.at[group, there],
                    third.at[group, d - 1],
                    send3.at[group, d - 1],
                    recv3.at[group, d - 1],
                    there * 4 + side * 2 + core,
                )
            )

    for step in range(PARTS + lags[1]):
        if step < PARTS:
            begin(step)
        if 0 <= step - lags[0] < PARTS:
            over_x(step - lags[0])
        if step >= lags[1]:
            over_rest(step - lags[1])
    for group in range(2):
        value = block[group, outer].astype(jnp.float32)
        for d in range(1, outers):
            copies3[group * (outers - 1) + d - 1].wait_recv()
            value = value + third[group, d - 1].astype(jnp.float32)
        finish(group, value)
    for copy in [*copies1.values(), *copies2.values(), *copies3]:
        copy.wait_send()


def sum_scratch(n, width):
    rows, outers = SLOT * n, n // 4
    dma = pltpu.SemaphoreType.DMA
    return [
        pltpu.VMEM((PARTS, rows, width), jnp.float32),
        pltpu.VMEM((PARTS, rows, width), jnp.bfloat16),
        pltpu.VMEM((PARTS, rows // 2, width), jnp.bfloat16),
        pltpu.VMEM((PARTS, rows // 2, width), jnp.bfloat16),
        pltpu.VMEM((PARTS, rows // 4, width), jnp.bfloat16),
        pltpu.VMEM((2, outers, 16, width), jnp.bfloat16),
        pltpu.VMEM((2, outers - 1, 16, width), jnp.bfloat16),
        dma((PARTS,)),
        dma((PARTS,)),
        dma((PARTS,)),
        dma((PARTS,)),
        dma((2, outers - 1)),
        dma((2, outers - 1)),
    ]


def project_kernel(
    n, heads_ref, weight_ref, out_ref, arrived, lhs, weight, send_sem, recv_sem, load_sem, *rest
):
    me, core, side, outer, slot = place(n)
    width = out_ref.shape[2]
    quarter = heads_ref.shape[2]
    loads = []
    for part in range(PARTS):
        load = pltpu.make_async_copy(
            weight_ref.at[:, pl.ds(part * width, width)], weight.at[part], load_sem.at[part]
        )
        load.start()
        loads.append(load)
    greet([lax.rem(me + d, n) for d in range(1, n)])
    copies = []
    for d in range(1, n):
        other = lax.rem(me + d, n)
        copies.append(
            send(
                heads_ref.at[other],
                arrived.at[slot],
                send_sem.at[d - 1],
                recv_sem.at[d - 1],
                other,
            )
        )
    arrived[slot] = heads_ref[me]
    for copy in copies:
        copy.wait_recv()
    rows = arrived[...].reshape(16 * n, quarter)
    for q in range(4):
        lhs[q] = jnp.dot(row_picker(n, q), rows, preferred_element_type=jnp.float32).astype(
            jnp.bfloat16
        )

    def product(part):
        loads[part].wait()
        total = jnp.zeros((SLOT * n, width), jnp.float32)
        for q in range(4):
            total = total + jnp.dot(
                lhs[q],
                weight[part, pl.ds(q * quarter, quarter)],
                preferred_element_type=jnp.float32,
            )
        return total

    def finish(group, value):
        out_ref[group] = value

    scatter_sum(n, product, finish, (3, 6), *rest[:7], rest[7:])
    for copy in copies:
        copy.wait_send()


def expert_kernel(
    n, summed_ref, resid_ref, gain_ref, tag_ref, gate_ref, up_ref, down_ref, out_ref,
    hidden, gathered, gate, up, down, load_sem, send_a, recv_a, send_b, recv_b, send_c, recv_c, *rest
):
    me, core, side, outer, slot = place(n)
    width = out_ref.shape[2]
    outers = n // 4
    loads = []
    for i, (src, dst) in enumerate(((gate_ref, gate), (up_ref, up), (down_ref, down))):
        load = pltpu.make_async_copy(src, dst, load_sem.at[i])
        load.start()
        loads.append(load)
    across, sibling = me + 2 - 4 * side, me + 1 - 2 * core
    peers = [lax.rem(outer + d, outers) * 4 + side * 2 + core for d in range(1, outers)]
    greet([*peers, across, sibling])
    squares = jnp.zeros((16, 1), jnp.float32)
    for group in range(2):
        value = summed_ref[group] + resid_ref[group]
        hidden[group] = value
        squares = squares + jnp.sum(value * value, axis=1, keepdims=True)
    total = squares[0:4] + squares[4:8] + squares[8:12] + squares[12:16]
    scale = lax.rsqrt(total / (PARTS * width) + norm_eps)
    scale = jnp.concatenate([scale] * 4, axis=0)
    for group in range(2):
        normed = (hidden[group] * scale * gain_ref[group]).astype(jnp.bfloat16)
        gathered[slot, group] = normed + tag_ref[group]
    mine = gathered.at[slot]
    along = []
    for d in range(1, outers):
        along.append(
            send(mine, mine, send_a.at[d - 1], recv_a.at[d - 1], peers[d - 1])
        )
    over, core_copies = [], []
    for d in range(outers):
        if d:
            along[d - 1].wait_recv()
        index = core * (n // 2) + side * (n // 4) + lax.rem(outer - d + outers, outers)
        held = gathered.at[index]
        over.append(send(held, held, send_b.at[d], recv_b.at[d], across))
        core_copies.append(send(held, held, send_c.at[d], recv_c.at[d], sibling))
    for d in range(outers):
        over[d].wait_recv()
        index = core * (n // 2) + (1 - side) * (n // 4) + lax.rem(outer - d + outers, outers)
        held = gathered.at[index]
        core_copies.append(
            send(held, held, send_c.at[outers + d], recv_c.at[outers + d], sibling)
        )
    for copy in core_copies:
        copy.wait_recv()
    loads[0].wait()
    loads[1].wait()
    gate_val = jnp.zeros((SLOT * n, gate.shape[1]), jnp.float32)
    up_val = jnp.zeros((SLOT * n, gate.shape[1]), jnp.float32)
    for part in range(PARTS):
        rows = gathered[:, part // 4].reshape(16 * n, width)
        lhs = jnp.dot(
            row_picker(n, part % 4), rows, preferred_element_type=jnp.float32
        ).astype(jnp.bfloat16)
        span = pl.ds(part * width, width)
        gate_val = gate_val + jnp.dot(lhs, gate[span], preferred_element_type=jnp.float32)
        up_val = up_val + jnp.dot(lhs, up[span], preferred_element_type=jnp.float32)
    row = lax.broadcasted_iota(jnp.int32, (SLOT * n, 16 * n), 0)
    col = lax.broadcasted_iota(jnp.int32, (SLOT * n, 16 * n), 1)
    tags = jnp.dot(
        (col == ((row >> 2) << 4) + 3).astype(jnp.bfloat16),
        gathered[:, 0].reshape(16 * n, width)[:, : 2 * LANES],
        preferred_element_type=jnp.float32,
    )
    row = lax.broadcasted_iota(jnp.int32, (SLOT * n, 2 * LANES), 0)
    col = lax.broadcasted_iota(jnp.int32, (SLOT * n, 2 * LANES), 1)
    wanted = (col & (LANES - 1)) == (me // SPLIT) * SLOT + (row & 3)
    coeff = jnp.sum(jnp.where(wanted, tags, 0.0), axis=1, keepdims=True)
    active = (gate_val / (1.0 + jnp.exp(-gate_val)) * up_val).astype(jnp.bfloat16)
    loads[2].wait()

    def product(part):
        value = jnp.dot(
            active, down[:, pl.ds(part * width, width)], preferred_element_type=jnp.float32
        )
        return jnp.where(coeff != 0.0, value * coeff, 0.0)

    def finish(group, value):
        out_ref[group] = (hidden[group] + value).astype(jnp.bfloat16)

    scatter_sum(n, product, finish, (PARTS, 2 * PARTS), *rest[:7], rest[7:])
    for copy in [*along, *over, *core_copies]:
        copy.wait_send()


def fold(value):
    seq_count, model_width = value.shape
    width = model_width // PARTS
    padded = jnp.pad(value, ((0, SLOT - seq_count), (0, 0)))
    return padded.reshape(SLOT, 2, 4, width).transpose(1, 2, 0, 3).reshape(2, 16, width)


def unfold(summed, seq_count):
    width = summed.shape[2]
    split = summed.reshape(2, 4, SLOT, width).transpose(2, 0, 1, 3)
    return split.reshape(SLOT, PARTS * width)[:seq_count]


def project(flat_heads, weight):
    n = lax.axis_size("ep")
    depth, model_width = weight.shape
    seq_count = flat_heads.shape[0]
    quarter, width = depth // 4, model_width // PARTS
    padded = jnp.pad(flat_heads, ((0, SLOT - seq_count), (0, 0)))
    blocks = padded.reshape(SLOT, n, 4, quarter).transpose(1, 2, 0, 3).reshape(n, 16, quarter)
    vmem = pl.BlockSpec(memory_space=pltpu.VMEM)
    dma = pltpu.SemaphoreType.DMA
    summed = pl.pallas_call(
        functools.partial(project_kernel, n),
        out_shape=jax.ShapeDtypeStruct((2, 16, width), jnp.float32),
        in_specs=[vmem, pl.BlockSpec(memory_space=pl.ANY)],
        out_specs=vmem,
        scratch_shapes=[
            pltpu.VMEM((n, 16, quarter), jnp.bfloat16),
            pltpu.VMEM((4, SLOT * n, quarter), jnp.bfloat16),
            pltpu.VMEM((PARTS, depth, width), jnp.bfloat16),
            dma((n - 1,)),
            dma((n - 1,)),
            dma((PARTS,)),
            *sum_scratch(n, width),
        ],
        compiler_params=pltpu.CompilerParams(
            collective_id=0, has_side_effects=True, vmem_limit_bytes=56 * 2**20
        ),
    )(blocks, weight)
    return summed


def experts(summed, resid, norm_gain, spread, w_gate, w_up, w_down):
    n = lax.axis_size("ep")
    seq_count, model_width = resid.shape
    hidden_width = w_gate.shape[1]
    width = model_width // PARTS
    outers = n // 4
    gain = jnp.repeat(norm_gain.reshape(2, 4, width), SLOT, axis=1)
    weights = jnp.pad(spread.T, ((0, 0), (0, SLOT - seq_count))).reshape(-1)
    weights = jnp.pad(weights, (0, LANES - weights.shape[0]))
    high = lax.reduce_precision(weights, 8, 7)
    tag_row = jnp.concatenate([high, weights - high]).astype(jnp.bfloat16)
    tags = jnp.pad(tag_row[None, None, :], ((0, 1), (3, 12), (0, width - 2 * LANES)))
    vmem = pl.BlockSpec(memory_space=pltpu.VMEM)
    hbm = pl.BlockSpec(memory_space=pl.ANY)
    dma = pltpu.SemaphoreType.DMA
    mixed = pl.pallas_call(
        functools.partial(expert_kernel, n),
        out_shape=jax.ShapeDtypeStruct((2, 16, width), jnp.bfloat16),
        in_specs=[vmem, vmem, vmem, vmem, hbm, hbm, hbm],
        out_specs=vmem,
        scratch_shapes=[
            pltpu.VMEM((2, 16, width), jnp.float32),
            pltpu.VMEM((n, 2, 16, width), jnp.bfloat16),
            pltpu.VMEM((model_width, hidden_width), jnp.bfloat16),
            pltpu.VMEM((model_width, hidden_width), jnp.bfloat16),
            pltpu.VMEM((hidden_width, model_width), jnp.bfloat16),
            dma((3,)),
            dma((outers - 1,)),
            dma((outers - 1,)),
            dma((outers,)),
            dma((outers,)),
            dma((2 * outers,)),
            dma((2 * outers,)),
            *sum_scratch(n, width),
        ],
        compiler_params=pltpu.CompilerParams(
            collective_id=1, has_side_effects=True, vmem_limit_bytes=56 * 2**20
        ),
    )(summed, fold(resid.astype(jnp.float32)), gain, tags, w_gate, w_up, w_down)
    return unfold(mixed, seq_count)


def local(
    resid,
    q_latent,
    q_rope,
    cache_latent,
    cache_rope,
    lengths,
    proj_weight,
    norm_gain,
    expert_ids,
    affinity,
    w_gate,
    w_up,
    w_down,
):
    seq_count = resid.shape[0]
    ctx_len = cache_latent.shape[1]
    devices = lax.axis_size("ep")
    experts_all = devices // SPLIT
    route_weight = route_factor * affinity / jnp.sum(affinity, axis=1, keepdims=True)
    expert_cols = jnp.arange(experts_all, dtype=jnp.int32)
    named = expert_ids[:, :, None] == expert_cols
    spread = jnp.sum(jnp.where(named, route_weight[:, :, None], 0.0), axis=1)
    scores = jnp.einsum("thc,tlc->thl", q_latent, cache_latent, preferred_element_type=jnp.float32)
    scores = (
        scores + jnp.einsum("thr,tlr->thl", q_rope, cache_rope, preferred_element_type=jnp.float32)
    ) * score_scale
    positions = jnp.arange(ctx_len, dtype=jnp.int32)
    valid_mask = positions[None, None, :] < lengths[:, None, None]
    scores = jnp.where(valid_mask, scores, -1e30)
    peak_score = jnp.max(scores, axis=2, keepdims=True)
    exponent = jnp.where(valid_mask, jnp.exp(scores - peak_score), 0.0)
    attention_weight = (exponent / jnp.sum(exponent, axis=2, keepdims=True)).astype(jnp.bfloat16)
    heads_out = jnp.einsum(
        "thl,tlc->thc", attention_weight, cache_latent, preferred_element_type=jnp.float32
    ).astype(jnp.bfloat16)
    flat_heads = heads_out.reshape(seq_count, -1)
    summed = project(flat_heads, proj_weight)
    return experts(summed, resid, norm_gain, spread, w_gate[0], w_up[0], w_down[0])


def solution(mesh):
    placed = (
        P(("grp", "ep"), None),
        P(("grp", "ep"), None, None),
        P(("grp", "ep"), None, None),
        P(("grp", "ep"), None, None),
        P(("grp", "ep"), None, None),
        P(("grp", "ep")),
        P("ep", None),
        P(),
        P(("grp", "ep"), None),
        P(("grp", "ep"), None),
        P("ep", None, None),
        P("ep", None, None),
        P("ep", None, None),
    )
    return jax.shard_map(
        local, mesh=mesh, in_specs=placed, out_specs=P(("grp", "ep"), None), check_vma=False
    )
```
